128 devices in a mesh: expert: 32 (over x, z, core), tensor: 4 (over y).
Axes of the slice: x: 4, y: 4, z: 4, core: 2. Of those that a mesh axis runs over, the one named last changes fastest.
Arguments:
- attn_partials: bfloat16 [4, 4096, 7168], P('tensor', 'expert'), may hold values from -3 to 3
- residual: bfloat16 [4096, 7168], P('expert'), may hold values from -22.05 to 22.05
- norm_gain: float32 [7168], P('tensor'), may hold values from 0.1 to 1.9
- gate_up: bfloat16 [64, 7168, 2048], P('expert', 'tensor'), may hold values from -0.0625 to 0.0625
- down: bfloat16 [64, 1024, 7168], P('expert', None, 'tensor'), may hold values from -0.1875 to 0.1875
- expert_ids: int32 [4096, 8], P('expert'), may hold values from 0 to 63, as said below
- gate_ints: int32 [4096, 8], P('expert'), may hold values from 2048 to 4096
Outputs:
- layer_out: bfloat16 [4096, 7168], P('expert', 'tensor')
The draws below stay inside these ranges and needn't reach their ends.
Inputs may be any that keep to these rules, and one draw needn't show every extreme that they name: `expert_ids`: each row names 8 different experts; among the 128 rows of one index of the expert axis no expert is named more than 24 times, and some expert is named exactly 24 times.
All inputs are finite; a program needn't handle non-finite values.
Results may differ from the reference program's by a relative error of at most 0.028.
Values may be sent and summed in bfloat16 or wider, within the bound.
A program may use at most 192 MiB of HBM per device.

```python
import math
import jax
import jax.numpy as jnp
from jax import lax

D = 7168
FF = 1024
TOPK = 8
EXP_DEV = 2
TOK_DEV = 128
EXPERTS = 64
TOKENS = 4096
CAP = 24
N_EXPERT = 32
N_TENSOR = 4


def draw_residual(key, part):
    key_base, key_col, key_row = jax.random.split(key, 3)
    column = jnp.arange(D, dtype=jnp.float32) / D
    ramp = 0.25 + 1.5 * column
    col_scale = jnp.exp(jax.random.uniform(key_col, (D,), jnp.float32, math.log(0.4), math.log(4.0)))
    row_scale = jnp.exp(jax.random.uniform(key_row, (TOKENS, 1), jnp.float32, math.log(0.3), math.log(3.0)))
    base = jnp.clip(jax.random.normal(key_base, (TOKENS, D), jnp.float32), -5.0, 5.0)
    values = 0.21 * base * ramp[None, :] * col_scale[None, :] * row_scale
    return values.astype(jnp.bfloat16)


def route_block(block_key, steady_device):
    key_devices, key_spread, key_rows = jax.random.split(block_key, 3)
    device_count = EXPERTS // EXP_DEV
    order_devices = jax.random.permutation(key_devices, device_count).astype(jnp.int32)
    position = jnp.argmax((order_devices == steady_device).astype(jnp.int32)).astype(jnp.int32)
    leading = order_devices[0]
    order_devices = order_devices.at[position].set(leading).at[0].set(steady_device)
    expert_order = (order_devices[:, None] * EXP_DEV + jnp.arange(EXP_DEV, dtype=jnp.int32)[None, :]).reshape(-1)
    crowded_count = device_count // 2 * EXP_DEV
    drawn_count = EXPERTS - crowded_count
    total_pairs = TOK_DEV * TOPK
    remaining = total_pairs - crowded_count * CAP
    baseline = remaining // drawn_count
    leftover = remaining - baseline * drawn_count
    spread = jax.random.randint(key_spread, (drawn_count // 2,), -baseline, baseline + 1).astype(jnp.int32)
    filler = jnp.zeros((drawn_count - 2 * (drawn_count // 2),), jnp.int32)
    shifts = jnp.concatenate([spread, -spread, filler], 0)
    drawn_loads = baseline + shifts + (jnp.arange(drawn_count, dtype=jnp.int32) < leftover).astype(jnp.int32)
    loads = jnp.concatenate([jnp.full((crowded_count,), CAP, jnp.int32), drawn_loads], 0)
    ends = jnp.cumsum(loads).astype(jnp.int32)
    label_index = jnp.arange(total_pairs, dtype=jnp.int32)
    internal = jnp.sum((label_index[:, None] >= ends[None, :]).astype(jnp.int32), axis=1)
    labels = expert_order[internal]
    table = labels.reshape(TOPK, TOK_DEV).T
    row_order = jax.random.permutation(key_rows, TOK_DEV).astype(jnp.int32)
    return table[row_order]


def draw_expert_ids(key, part):
    key = jax.random.fold_in(key, 11)
    device_count = EXPERTS // EXP_DEV
    steady_device = jax.random.randint(jax.random.fold_in(key, 0), (), 0, device_count).astype(jnp.int32)
    block_keys = jax.random.split(jax.random.fold_in(key, 1), N_EXPERT)
    blocks = jax.vmap(lambda block_key: route_block(block_key, steady_device))(block_keys)
    return blocks.reshape(TOKENS, TOPK).astype(jnp.int32)


def set_ends(values, own_key, smallest, high):
    longest = values.shape.index(max(values.shape))
    spots = []
    for shift in (0, 1):
        where = [jax.random.randint(jax.random.fold_in(own_key, axis), (), 0, length) for axis, length in enumerate(values.shape)]
        where[longest] = (where[longest] + shift) % values.shape[longest]
        spots.append(tuple(where))
    return values.at[spots[0]].set(smallest).at[spots[1]].set(high)


def with_spikes(entries, stream_key, source, target, shards_of, factor):
    def block_of(axis_at):
        return (jnp.arange(entries.shape[axis_at]) // (entries.shape[axis_at] // shards_of)).reshape((-1,) + (1,) * (entries.ndim - 1 - axis_at))

    one_side = jax.random.permutation(stream_key, shards_of)[block_of(target)]
    other_side = (block_of(target) + shards_of // 2) % shards_of
    return jnp.where((block_of(source) == one_side) | (block_of(source) == other_side), factor * entries, entries)


def block_levels(stream_key, extent, cuts, smallest, high):
    gain, own = 1.0, jax.random.fold_in(stream_key, 6)
    for dim, parts in cuts:
        draws = jnp.exp(jax.random.uniform(jax.random.fold_in(own, dim), (parts,), jnp.float32, smallest / len(cuts), high / len(cuts)))
        gain = gain * jnp.repeat(draws, extent[dim] // parts).reshape([-1 if axis == dim else 1 for axis in range(len(extent))])
    return gain


def normal_values(stream_key, dims, scale, most, cuts=(), kind=jnp.bfloat16):
    values = scale * jax.random.normal(stream_key, dims, jnp.float32)
    if cuts:
        values = values * block_levels(stream_key, dims, cuts, -0.22, 0.18)
    return jnp.clip(values, -most, most).astype(kind)


def noise_with(rng, shape, deviation, bound, shards, heavy, kind=jnp.bfloat16):
    entries = deviation * jax.random.normal(rng, shape, jnp.float32)
    if shards:
        entries = entries * block_levels(rng, shape, shards, -0.22, 0.18)
    return jnp.clip(with_spikes(entries, jax.random.fold_in(rng, 3), *heavy), -bound, bound).astype(kind)


def setup_inputs(seed: int = 0) -> dict:
    streams_of = jax.random.split(jax.random.key(seed), 8)
    return {
        "attn_partials": noise_with(streams_of[0], (N_TENSOR, TOKENS, D), 0.25, 3.0, ((0, 4), (1, 32)), (0, 2, 4, 2.0)),
        "residual": draw_residual(jax.random.fold_in(streams_of[7], 71), 0),
        "norm_gain": jnp.clip(1.0 + 0.18 * jax.random.normal(streams_of[2], (D,), jnp.float32), 0.1, 1.9),
        "gate_up": normal_values(streams_of[3], (EXPERTS, D, 2 * FF), D ** -0.5, 0.0625, ((0, 32), (1, 4))),
        "down": normal_values(streams_of[4], (EXPERTS, FF, D), FF ** -0.5, 0.1875, ((0, 32), (2, 4))),
        "expert_ids": draw_expert_ids(jax.random.fold_in(streams_of[7], 71), 0),
        "gate_ints": set_ends(jax.random.randint(streams_of[6], (TOKENS, TOPK), 2048, 4097), jax.random.fold_in(streams_of[6], 1), 2048, 4096).astype(jnp.int32),
    }


def reference(attn_partials, residual, norm_gain, gate_up, down, expert_ids, gate_ints):
    attention = lax.optimization_barrier(jnp.sum(attn_partials.astype(jnp.float32), axis=0))
    stream = (residual.astype(jnp.float32) + attention).astype(jnp.bfloat16)
    stream_wide = stream.astype(jnp.float32)
    mean_square = lax.optimization_barrier(jnp.mean(stream_wide * stream_wide, axis=1, keepdims=True))
    normed = (stream_wide * lax.rsqrt(mean_square + 1e-06) * norm_gain[None, :]).astype(jnp.bfloat16)
    gate_float = gate_ints.astype(jnp.float32)
    gates = 2.5 * gate_float / lax.optimization_barrier(jnp.sum(gate_float, axis=1, keepdims=True))
    quarter = D // N_TENSOR
    row_limit = N_EXPERT * CAP
    padded = jnp.concatenate([normed, jnp.zeros((1, D), jnp.bfloat16)], 0)

    def one_expert(carry, expert_index):
        matched = expert_ids == expert_index
        chosen = jnp.any(matched, axis=1)
        picked_rows = jnp.nonzero(chosen, size=row_limit, fill_value=TOKENS)[0].astype(jnp.int32)
        routed = padded[picked_rows]
        weight_gu = gate_up[expert_index]
        gate_total = jnp.zeros((row_limit, 2 * FF), jnp.float32)
        for part_index in range(N_TENSOR):
            part_sum = jnp.dot(routed[:, part_index * quarter:(part_index + 1) * quarter], weight_gu[part_index * quarter:(part_index + 1) * quarter], preferred_element_type=jnp.float32)
            rounded = lax.optimization_barrier(part_sum.astype(jnp.bfloat16))
            gate_total = gate_total + rounded.astype(jnp.float32)
        hidden = (jax.nn.silu(gate_total[:, :FF]) * gate_total[:, FF:]).astype(jnp.bfloat16)
        expert_out = jnp.dot(hidden, down[expert_index], preferred_element_type=jnp.float32).astype(jnp.bfloat16)
        row_gate = lax.optimization_barrier(jnp.sum(jnp.where(matched, gates, jnp.zeros_like(gates)), axis=1))
        row_gate = jnp.concatenate([row_gate, jnp.zeros((1,), jnp.float32)], 0)
        weighted = expert_out.astype(jnp.float32) * row_gate[picked_rows][:, None]
        return (carry.at[picked_rows].add(weighted), None)
    initial = jnp.zeros((TOKENS + 1, D), jnp.float32)
    routed_sum, _ = lax.scan(one_expert, initial, jnp.arange(EXPERTS, dtype=jnp.int32))
    return (stream_wide + routed_sum[:TOKENS]).astype(jnp.bfloat16)
```

```python
import functools
import jax
import jax.numpy as jnp
import numpy as np
from jax import lax
from jax.experimental import pallas as pl
from jax.experimental.pallas import tpu as pltpu
from jax.sharding import PartitionSpec as P

MESH = pl.DeviceIdType.MESH
F32, BF16 = jnp.float32, jnp.bfloat16
DZ = (0, 2, 1, 3)
STEP_DX = (0, 1, 3, 1, 3, 2, 2, 0)
STEP_PAIR = (1, 1, 1, 0, 0, 1, 0, 0)
STEPS = 8
META = 128


def lut(index, values):
    result = jnp.int32(values[0])
    for at, value in enumerate(values):
        if at:
            result = jnp.where(index == at, jnp.int32(value), result)
    return result


def row_table(cap):
    table = np.full((8, 8 * cap), -1e6, np.float32)
    for l in range(2):
        for q in range(2):
            for j in range(cap):
                for s in range(2):
                    table[2 * q + s, ((l * 2 + s) * 2 + q) * cap + j] = l * cap + j
                table[4 + q, (l * 2 + q) * cap + j] = l * cap + j
    return table


def layer_kernel(
    cap,
    attn,
    resid,
    gain,
    wgu,
    wdn,
    ids,
    ints,
    tab,
    out,
    wg,
    wd,
    toks,
    pb,
    xb,
    yr,
    hb,
    ob,
    pr,
    own,
    cs,
    zr,
    xr,
    ar,
    stream,
    ssb,
    w_sem,
    l_sem,
    ar_s,
    ar_r,
    ss_s,
    ss_r,
    agz_s,
    agx_s,
    ag_r,
    core_s,
    core_r,
    y_s,
    y_r,
    h_s,
    h_r,
    p_s,
    p_r,
    z_s,
    z_r,
    x_s,
    x_r,
):
    e = lax.axis_index("expert")
    y = lax.axis_index("tensor")
    x, z, c = e // 8, lax.rem(e // 2, 4), lax.rem(e, 2)
    tokens, quarter = stream.shape
    top = ids.shape[1]
    width = 4 * quarter
    half_rows = 4 * cap
    block = hb.shape[3]

    def at(dx=0, dz=0, dc=0, dy=0):
        ex = (lax.rem(x + dx, 4) * 4 + lax.rem(z + dz, 4)) * 2 + lax.rem(c + dc, 2)
        return (ex, lax.rem(y + dy, 4))

    def remote(src, dst, ssem, rsem, dev):
        return pltpu.make_async_remote_copy(
            src_ref=src, dst_ref=dst, send_sem=ssem, recv_sem=rsem, device_id=dev, device_id_type=MESH
        )

    def cols(start, size):
        return pl.ds(pl.multiple_of(start * size, size), size)

    def attn_copy(d):
        return remote(
            attn.at[:, cols(lax.rem(y + d, 4), quarter)], ar.at[d - 1], ar_s.at[d - 1], ar_r.at[d - 1], at(dy=d)
        )

    for d in (1, 3, 2):
        attn_copy(d).start()
    mine = pltpu.make_async_copy(attn.at[:, cols(y, quarter)], cs.at[0, 0], l_sem.at[0])
    rest = pltpu.make_async_copy(resid.at[:, cols(y, quarter)], cs.at[0, 1], l_sem.at[1])
    mine.start()
    rest.start()

    def weight_copies():
        copies = []
        for l in range(2):
            for o in range(4):
                for g in range(2):
                    copies.append(
                        pltpu.make_async_copy(
                            wgu.at[l, :, pl.ds(g * 4 * block + o * block, block)],
                            wg.at[l, o, :, pl.ds(g * block, block)],
                            w_sem.at[(l * 4 + o) * 2 + g],
                        )
                    )
            copies.append(pltpu.make_async_copy(wdn.at[l], wd.at[l], w_sem.at[16 + l]))
        return copies

    for copy in weight_copies():
        copy.start()

    lane = lax.broadcasted_iota(jnp.int32, (tokens, META), 1)
    row = lax.broadcasted_iota(jnp.int32, (tokens, META), 0)
    id_block = ids[...]
    hits = jnp.zeros((tokens, META), F32)
    for k in range(top):
        hits = hits + jnp.where(id_block[:, k : k + 1] == lane, 1.0, 0.0)
    before = jnp.where(lane < row, 1.0, 0.0).astype(BF16)
    count = jnp.dot(before, hits.astype(BF16), preferred_element_type=F32)
    gate_float = ints[...].astype(F32)
    gates = 2.5 * gate_float / jnp.sum(gate_float, axis=1, keepdims=True)
    meta = jnp.zeros((tokens, META), F32)
    for k in range(top):
        this = id_block[:, k : k + 1]
        slot = jnp.sum(jnp.where(this == lane, count, 0.0), axis=1, keepdims=True)
        meta = jnp.where(lane == k, this.astype(F32), meta)
        meta = jnp.where(lane == top + k, slot, meta)
        meta = jnp.where(lane == 2 * top + k, gates[:, k : k + 1], meta)
    toks[0, 0, c, :, pl.ds(quarter, META)] = meta.astype(BF16)

    mine.wait()
    rest.wait()
    for d in (1, 3, 2):
        attn_copy(d).wait_recv()
    attention = cs[0, 0].astype(F32) + ar[0].astype(F32) + ar[1].astype(F32) + ar[2].astype(F32)
    summed = (cs[0, 1].astype(F32) + attention).astype(BF16)
    stream[...] = summed
    wide = summed.astype(F32)
    ssb[0] = jnp.broadcast_to(jnp.sum(wide * wide, axis=1, keepdims=True), (tokens, META))

    def ss_copy(d):
        return remote(ssb.at[0], ssb.at[d], ss_s.at[d - 1], ss_r.at[d - 1], at(dy=d))

    for d in (1, 3, 2):
        ss_copy(d).start()
    for d in (1, 3, 2):
        ss_copy(d).wait_recv()
    total = (ssb[0] + ssb[1] + ssb[2] + ssb[3])[:, :1]
    wide = stream[...].astype(F32)
    normed = wide * lax.rsqrt(total / width + 1e-06) * gain[...]
    toks[0, 0, c, :, pl.ds(0, quarter)] = normed.astype(BF16)

    def agz_copy(p):
        dz = DZ[p]
        there = DZ.index((4 - dz) % 4)
        return remote(toks.at[0, 0, c], toks.at[0, there, c], agz_s.at[p], ag_r.at[0, there], at(dz=dz))

    def agx_copy(p, dx):
        return remote(toks.at[0, p, c], toks.at[4 - dx, p, c], agx_s.at[p, dx], ag_r.at[4 - dx, p], at(dx=dx))

    def arrival(dx, p):
        return remote(toks.at[dx, p, c], toks.at[dx, p, c], agz_s.at[0], ag_r.at[dx, p], at(dc=1))

    def core_copy(dx, p):
        return remote(toks.at[dx, p, c], toks.at[dx, p, c], core_s.at[dx, p], core_r.at[dx, p], at(dc=1))

    def core_arrival(dx, p):
        there = toks.at[dx, p, 1 - c]
        return remote(there, there, core_s.at[dx, p], core_r.at[dx, p], at(dc=1))

    agz_copy(2).start()
    agz_copy(3).start()
    agx_copy(0, 1).start()
    agx_copy(0, 3).start()
    agz_copy(1).start()
    for p in (2, 3):
        arrival(0, p).wait_recv()
        core_copy(0, p).start()
        agx_copy(p, 1).start()
        agx_copy(p, 3).start()
    for copy in weight_copies():
        copy.wait()

    def codes_of(dx, p, s):
        m = toks[dx, p, s, :, pl.ds(quarter, META)].astype(F32)
        return m[:, :top] * cap + m[:, top : 2 * top], m[:, 2 * top : 3 * top]

    def y_copy(j, d):
        return remote(
            pb.at[lax.rem(j, 2), lax.rem(y + d, 4)],
            yr.at[lax.rem(j, 4), d - 1],
            y_s.at[lax.rem(j, 2), d - 1],
            y_r.at[lax.rem(j, 4), d - 1],
            at(dy=d),
        )

    def h_copy(j, d):
        spot = hb.at[lax.rem(j, 4), y]
        return remote(spot, spot, h_s.at[lax.rem(j, 4), d - 1], h_r.at[lax.rem(j, 4), d - 1], at(dy=d))

    def h_arrival(j, d):
        spot = hb.at[lax.rem(j, 4), lax.rem(y + 4 - d, 4)]
        return remote(spot, spot, h_s.at[lax.rem(j, 4), d - 1], h_r.at[lax.rem(j, 4), d - 1], at(dy=d))

    def p_copy(j):
        return remote(
            ob.at[lax.rem(j, 2), :, 1 - c],
            pr.at[lax.rem(j, 4)],
            p_s.at[lax.rem(j, 2)],
            p_r.at[lax.rem(j, 4)],
            at(dc=1),
        )

    def z_copy(j, dx, q, dz):
        return remote(cs.at[lax.rem(j, 2), q], zr.at[dx, dz - 1], z_s.at[lax.rem(j, 2), q], z_r.at[dx, dz - 1], at(dz=dz))

    def x_copy(dx):
        return remote(own.at[dx], xr.at[dx - 1], x_s.at[dx - 1], x_r.at[dx - 1], at(dx=dx))

    def project(j):
        dx, p0 = lut(j, STEP_DX), 2 * lut(j, STEP_PAIR)
        core_arrival(dx, p0).wait_recv()
        core_arrival(dx, p0 + 1).wait_recv()
        picks = []
        for q in range(2):
            for s in range(2):
                codes, _ = codes_of(dx, p0 + q, s)
                rows = tab[2 * q + s : 2 * q + s + 1, :] + (2 * cap * e).astype(F32)
                pick = jnp.zeros((tokens, 8 * cap), F32)
                for k in range(top):
                    pick = jnp.where(codes[:, k : k + 1] == rows, 1.0, pick)
                picks.append(pick)
        pick = jnp.concatenate(picks, axis=0).astype(BF16)

        @pl.loop(0, quarter // 256)
        def _(n):
            data = toks[dx, pl.ds(p0, 2), :, :, cols(n, 256)].reshape(4 * tokens, 256)
            xb[:, cols(n, 256)] = lax.dot_general(
                pick, data, (((0,), (0,)), ((), ())), preferred_element_type=F32
            ).astype(BF16)

        for l in range(2):

            @pl.loop(0, 4)
            def _(o):
                pb[lax.rem(j, 2), o, pl.ds(l * half_rows, half_rows), :] = jnp.dot(
                    xb[pl.ds(l * half_rows, half_rows), :], wg[l, o], preferred_element_type=F32
                ).astype(BF16)

        for d in (1, 3, 2):
            y_copy(j, d).start()

    def service(j):
        dx, p0 = lut(j, STEP_DX), 2 * lut(j, STEP_PAIR)
        for q in range(2):

            @pl.when(dx != 0)
            def _():
                arrival(dx, p0 + q).wait_recv()

            core_copy(dx, p0 + q).start()

    def activate(j):
        for d in (1, 3, 2):
            y_copy(j, d).wait()
        slot = lax.rem(j, 4)
        value = pb[lax.rem(j, 2), y].astype(F32)
        for d in range(3):
            value = value + yr[slot, d].astype(F32)
        hb[slot, y] = (jax.nn.silu(value[:, :block]) * value[:, block:]).astype(BF16)
        for d in (1, 3, 2):
            h_copy(j, d).start()

    def expand(j):
        for d in (1, 3, 2):
            h_copy(j, d).wait_send()
            h_arrival(j, d).wait_recv()
        slot = lax.rem(j, 4)
        for l in range(2):

            @pl.loop(0, quarter // 256)
            def _(n):
                acc = jnp.zeros((half_rows, 256), F32)
                for o in range(4):
                    acc = acc + jnp.dot(
                        hb[slot, o, pl.ds(l * half_rows, half_rows), :],
                        wd[l, pl.ds(o * block, block), cols(n, 256)],
                        preferred_element_type=F32,
                    )
                ob[lax.rem(j, 2), l, :, :, cols(n, 256)] = acc.astype(BF16).reshape(2, 2 * cap, 256)

        p_copy(j).start()

    def gather_back(j):
        dx, pair = lut(j, STEP_DX), lut(j, STEP_PAIR)
        p_copy(j).wait()

        @pl.when(j >= 2)
        def _():
            before_pair = lut(j - 2, STEP_PAIR)

            @pl.when(before_pair == 1)
            def _():
                z_copy(j, 0, 0, 1).wait_send()

            z_copy(j, 0, 1, 1).wait_send()

        for q in range(2):
            codes, gate = codes_of(dx, 2 * pair + q, c)
            sides = []
            for base in (e, e + 1 - 2 * c):
                rows = tab[4 + q : 5 + q, : 4 * cap] + (2 * cap * base).astype(F32)
                side = jnp.zeros((tokens, 4 * cap), F32)
                for k in range(top):
                    side = jnp.where(codes[:, k : k + 1] == rows, gate[:, k : k + 1], side)
                sides.append(side.astype(BF16))

            def block_of(n):
                here = ob[lax.rem(j, 2), :, c, :, cols(n, 256)].reshape(4 * cap, 256)
                other = pr[lax.rem(j, 4), :, :, cols(n, 256)].reshape(4 * cap, 256)
                value = jnp.dot(sides[0], here, preferred_element_type=F32)
                return (value + jnp.dot(sides[1], other, preferred_element_type=F32)).astype(BF16)

            if q == 0:

                @pl.when(pair == 0)
                def _():
                    @pl.loop(0, quarter // 256)
                    def _(n):
                        own[dx, :, cols(n, 256)] = block_of(n)

                @pl.when(pair == 1)
                def _():
                    @pl.loop(0, quarter // 256)
                    def _(n):
                        cs[lax.rem(j, 2), 0, :, cols(n, 256)] = block_of(n)

                    z_copy(j, dx, 0, 1).start()

            else:

                @pl.loop(0, quarter // 256)
                def _(n):
                    cs[lax.rem(j, 2), 1, :, cols(n, 256)] = block_of(n)

                z_copy(j, dx, 1, jnp.where(pair == 0, 2, 3)).start()

    def combine(dx):
        value = own[dx].astype(F32)
        for dz in (1, 2, 3):
            remote(zr.at[dx, dz - 1], zr.at[dx, dz - 1], z_s.at[0, 0], z_r.at[dx, dz - 1], at(dz=dz)).wait_recv()
            value = value + zr[dx, dz - 1].astype(F32)
        return value

    @pl.loop(0, STEPS + 3)
    def _(it):
        @pl.when(it < STEPS)
        def _():
            project(it)

        @pl.when(it == 0)
        def _():
            arrival(0, 1).wait_recv()
            agx_copy(1, 1).start()
            agx_copy(1, 3).start()

        @pl.when(it == 1)
        def _():
            agx_copy(2, 2).start()

        @pl.when(it == 2)
        def _():
            agx_copy(3, 2).start()

        @pl.when(it == 3)
        def _():
            agx_copy(0, 2).start()
            agx_copy(1, 2).start()

        @pl.when(it + 1 < STEPS)
        def _():
            service(it + 1)

        @pl.when((it >= 1) & (it <= STEPS))
        def _():
            activate(it - 1)

        @pl.when((it >= 2) & (it <= STEPS + 1))
        def _():
            expand(it - 2)

        @pl.when(it >= 3)
        def _():
            gather_back(it - 3)

        @pl.when(it >= 8)
        def _():
            dx = lut(it - 8, (1, 3, 2))
            own[dx] = combine(dx).astype(BF16)
            x_copy(dx).start()

    value = stream[...].astype(F32) + combine(0)
    for dx in (1, 3, 2):
        x_copy(dx).wait()
        value = value + xr[dx - 1].astype(F32)
    out[...] = value.astype(BF16)

    for d in (1, 2, 3):
        attn_copy(d).wait_send()
        ss_copy(d).wait_send()
    for p in (1, 2, 3):
        agz_copy(p).wait_send()
    for p in range(4):
        for dx in range(4):
            if dx:
                agx_copy(p, dx).wait_send()
            core_copy(dx, p).wait_send()
    for j in (STEPS - 2, STEPS - 1):
        z_copy(j, 0, 1, 1).wait_send()


def per_device(attn_partials, residual, norm_gain, gate_up, down, expert_ids, gate_ints):
    tokens, width = residual.shape
    quarter = norm_gain.shape[0]
    local, _, double = gate_up.shape
    hidden = down.shape[1]
    block = hidden // 4
    groups = lax.axis_size("expert")
    top = expert_ids.shape[1]
    cap = 3 * tokens * top // (2 * groups * local)
    rows = 8 * cap
    dma = pltpu.SemaphoreType.DMA
    vmem = pl.BlockSpec(memory_space=pltpu.VMEM)
    anywhere = pl.BlockSpec(memory_space=pl.ANY)
    scratch = [
        pltpu.VMEM((local, 4, quarter, 2 * block), BF16),
        pltpu.VMEM((local, hidden, quarter), BF16),
        pltpu.VMEM((4, 4, 2, tokens, quarter + META), BF16),
        pltpu.VMEM((2, 4, rows, 2 * block), BF16),
        pltpu.VMEM((rows, quarter), BF16),
        pltpu.VMEM((4, 3, rows, 2 * block), BF16),
        pltpu.VMEM((4, 4, rows, block), BF16),
        pltpu.VMEM((2, local, 2, 2 * cap, quarter), BF16),
        pltpu.VMEM((4, local, 2 * cap, quarter), BF16),
        pltpu.VMEM((4, tokens, quarter), BF16),
        pltpu.VMEM((2, 2, tokens, quarter), BF16),
        pltpu.VMEM((4, 3, tokens, quarter), BF16),
        pltpu.VMEM((3, tokens, quarter), BF16),
        pltpu.VMEM((3, tokens, quarter), BF16),
        pltpu.VMEM((tokens, quarter), BF16),
        pltpu.VMEM((4, tokens, META), F32),
        dma((18,)),
        dma((2,)),
        dma((3,)),
        dma((3,)),
        dma((3,)),
        dma((3,)),
        dma((4,)),
        dma((4, 4)),
        dma((4, 4)),
        dma((4, 4)),
        dma((4, 4)),
        dma((2, 3)),
        dma((4, 3)),
        dma((4, 3)),
        dma((4, 3)),
        dma((2,)),
        dma((4,)),
        dma((2, 2)),
        dma((4, 3)),
        dma((3,)),
        dma((3,)),
    ]
    return pl.pallas_call(
        functools.partial(layer_kernel, cap),
        out_shape=jax.ShapeDtypeStruct((tokens, quarter), BF16),
        in_specs=[anywhere, anywhere, vmem, anywhere, anywhere, vmem, vmem, vmem],
        out_specs=vmem,
        scratch_shapes=scratch,
        compiler_params=pltpu.CompilerParams(has_side_effects=True, vmem_limit_bytes=62 * 2**20),
        cost_estimate=pl.CostEstimate(flops=30 * 10**9, bytes_accessed=30 * 10**6, transcendentals=0),
    )(
        attn_partials[0],
        residual,
        norm_gain[None, :],
        gate_up,
        down,
        expert_ids,
        gate_ints,
        jnp.asarray(row_table(cap)),
    )


def solution(mesh):
    in_specs = (
        P("tensor", "expert", None),
        P("expert", None),
        P("tensor"),
        P("expert", "tensor", None),
        P("expert", None, "tensor"),
        P("expert", None),
        P("expert", None),
    )
    return jax.shard_map(
        per_device, mesh=mesh, in_specs=in_specs, out_specs=P("expert", "tensor"), check_vma=False
    )
```

```python
import functools
import jax
import jax.numpy as jnp
import numpy as np
from jax import lax
from jax.experimental import pallas as pl
from jax.experimental.pallas import tpu as pltpu
from jax.sharding import PartitionSpec as P

MESH = pl.DeviceIdType.MESH
F32, BF16 = jnp.float32, jnp.bfloat16
CHIP_DX = (0, 0, 1, 3, 1, 3, 1, 3, 2, 2, 1, 3, 2, 2, 0, 0)
CHIP_DZ = (1, 3, 0, 0, 1, 3, 3, 1, 1, 3, 2, 2, 0, 2, 0, 2)
STEPS = 8
META = 128


def lut(index, values):
    result = jnp.int32(values[0])
    for at, value in enumerate(values):
        if at:
            result = jnp.where(index == at, jnp.int32(value), result)
    return result


def row_table(cap):
    table = np.full((8, 4 * cap), -1e6, np.float32)
    for l in range(2):
        for q in range(2):
            for j in range(cap):
                table[q, (l * 2 + q) * cap + j] = l * cap + j
    return table


def layer_kernel(
    cap,
    experts_all,
    attn,
    resid,
    gain,
    wgu,
    wdn,
    ids,
    ints,
    tab,
    out,
    wg,
    wd,
    toks,
    rowc,
    pb,
    xb,
    y1,
    y2,
    hb,
    ob,
    pr,
    own,
    cs,
    fr,
    sr,
    stream,
    ssb,
    w_sem,
    l_sem,
    a1_s,
    a1_r,
    a2_s,
    a2_r,
    ss_s,
    ss_r,
    ag1_s,
    ag1_r,
    ag2_s,
    ag2_r,
    agf_s,
    agf_r,
    core_s,
    core_r,
    y1_s,
    y1_r,
    y2_s,
    y2_r,
    h_s,
    h_r,
    p_s,
    p_r,
    f_s,
    f_r,
    s_s,
    s_r,
):
    e = lax.axis_index("expert")
    y = lax.axis_index("tensor")
    x, z, c = e // 8, lax.rem(e // 2, 4), lax.rem(e, 2)
    tokens, quarter = stream.shape
    top = ids.shape[0]
    width = 4 * quarter
    half_rows = 4 * cap
    block = hb.shape[3]

    def at(dx=0, dz=0, dc=0, dy=0):
        ex = (lax.rem(x + dx, 4) * 4 + lax.rem(z + dz, 4)) * 2 + lax.rem(c + dc, 2)
        return (ex, lax.rem(y + dy, 4))

    def remote(src, dst, ssem, rsem, dev):
        return pltpu.make_async_remote_copy(
            src_ref=src, dst_ref=dst, send_sem=ssem, recv_sem=rsem, device_id=dev, device_id_type=MESH
        )

    def cols(start, size):
        return pl.ds(pl.multiple_of(start * size, size), size)

    barrier = pltpu.get_barrier_semaphore()
    peers = [at(dy=d) for d in (1, 2, 3)] + [at(dx=d) for d in (1, 2, 3)] + [at(dz=d) for d in (1, 2, 3)] + [at(dc=1)]
    for peer in peers:
        pl.semaphore_signal(barrier, inc=1, device_id=peer, device_id_type=MESH)
    pl.semaphore_wait(barrier, len(peers))

    half = tokens // 2

    def attn_first(side):
        rows = pl.ds(side * half, half)
        source = attn.at[rows, cols(lax.rem(y + 2, 4), quarter)]
        return remote(source, fr.at[1, 2, rows], a1_s.at[side], a1_r.at[side], at(dy=1 + 2 * side))

    def attn_second(side):
        return remote(cs.at[1, side], fr.at[1, side], a2_s.at[side], a2_r.at[side], at(dy=1 + 2 * side))

    attn_first(0).start()
    attn_first(1).start()
    beside = [
        pltpu.make_async_copy(attn.at[:, cols(lax.rem(y + 1 + 2 * side, 4), quarter)], cs.at[1, side], l_sem.at[side])
        for side in range(2)
    ]
    mine = pltpu.make_async_copy(attn.at[:, cols(y, quarter)], cs.at[0, 0], l_sem.at[2])
    rest = pltpu.make_async_copy(resid.at[:, cols(y, quarter)], cs.at[0, 1], l_sem.at[3])
    for copy in (*beside, mine, rest):
        copy.start()

    def weight_copies():
        copies = []
        for l in range(2):
            for o in range(4):
                for g in range(2):
                    copies.append(
                        pltpu.make_async_copy(
                            wgu.at[l, :, pl.ds(g * 4 * block + o * block, block)],
                            wg.at[l, o, :, pl.ds(g * block, block)],
                            w_sem.at[(l * 4 + o) * 2 + g],
                        )
                    )
            copies.append(pltpu.make_async_copy(wdn.at[l], wd.at[l], w_sem.at[16 + l]))
        return copies

    for copy in weight_copies():
        copy.start()
    for side in range(2):
        rows = pl.ds(side * half, half)
        beside[side].wait()
        attn_first(side).wait_recv()
        value = cs[1, side, rows, :].astype(F32) + fr[1, 2, rows, :].astype(F32)
        cs[1, side, rows, :] = value.astype(BF16)
        attn_second(side).start()

    experts = lax.broadcasted_iota(jnp.int32, (experts_all, tokens), 0)
    pick_row = lax.broadcasted_iota(jnp.int32, (top, tokens), 0)
    id_block = ids[...]
    hits = jnp.zeros((experts_all, tokens), F32)
    for k in range(top):
        hits = hits + jnp.where(id_block[k : k + 1, :] == experts, 1.0, 0.0)
    earlier = lax.broadcasted_iota(jnp.int32, (tokens, tokens), 0) < lax.broadcasted_iota(jnp.int32, (tokens, tokens), 1)
    count = jnp.dot(hits.astype(BF16), jnp.where(earlier, 1.0, 0.0).astype(BF16), preferred_element_type=F32)
    slots = jnp.zeros((top, tokens), F32)
    for k in range(top):
        slot = jnp.sum(jnp.where(id_block[k : k + 1, :] == experts, count, 0.0), axis=0, keepdims=True)
        slots = jnp.where(pick_row == k, slot, slots)
    gate_float = ints[...].astype(F32)
    gates = 2.5 * gate_float / jnp.sum(gate_float, axis=0, keepdims=True)
    rest_rows = jnp.zeros((META - 3 * top, tokens), F32)
    meta = jnp.concatenate([id_block.astype(F32), slots, gates, rest_rows], axis=0)
    toks[0, 0, c, :, pl.ds(quarter, META)] = meta.T.astype(BF16)

    r = lax.broadcasted_iota(jnp.int32, (8 * cap, tokens), 0)
    l_of = (r >= 4 * cap).astype(jnp.int32)
    r = r - 4 * cap * l_of
    s_of = (r >= 2 * cap).astype(jnp.int32)
    r = r - 2 * cap * s_of
    q_of = (r >= cap).astype(jnp.int32)
    code = (r - cap * q_of + cap * l_of + 2 * cap * e).astype(F32)
    for q in range(2):
        for s in range(2):
            rowc[2 * q + s] = jnp.where((q_of == q) & (s_of == s), code, -1e6)

    mine.wait()
    rest.wait()
    attn_second(0).wait_recv()
    attn_second(1).wait_recv()
    attention = cs[0, 0].astype(F32) + fr[1, 0].astype(F32) + fr[1, 1].astype(F32)
    summed = (cs[0, 1].astype(F32) + attention).astype(BF16)
    stream[...] = summed
    wide = summed.astype(F32)
    ssb[0] = jnp.broadcast_to(jnp.sum(wide * wide, axis=1, keepdims=True), (tokens, META))

    def ss_copy(d):
        return remote(ssb.at[0], ssb.at[d], ss_s.at[d - 1], ss_r.at[d - 1], at(dy=d))

    for d in (1, 3, 2):
        ss_copy(d).start()
    for d in (1, 3, 2):
        ss_copy(d).wait_recv()
    total = (ssb[0] + ssb[1] + ssb[2] + ssb[3])[:, :1]
    wide = stream[...].astype(F32)
    normed = wide * lax.rsqrt(total / width + 1e-06) * gain[...].reshape(1, quarter)
    toks[0, 0, c, :, pl.ds(0, quarter)] = normed.astype(BF16)

    def turned(a, b):
        return a * c + b * (1 - c), a * (1 - c) + b * c

    def spot(a, b):
        dx, dz = turned(a, b)
        return toks.at[dx, dz, c]

    def toward(a, b):
        dx, dz = turned(a, b)
        return at(dx=dx, dz=dz)

    def ag_first(a):
        return remote(spot(0, 0), spot(4 - a, 0), ag1_s.at[a], ag1_r.at[4 - a], toward(a, 0))

    def ag_second(a, b):
        return remote(spot(a, 0), spot(a, 4 - b), ag2_s.at[a, b], ag2_r.at[a, 4 - b], toward(0, b))

    def pass_on(a, side):
        rows = pl.ds(side * half, half)
        return remote(
            spot(a, 3 - 2 * side).at[rows],
            spot(a, 2).at[rows],
            agf_s.at[a, side],
            agf_r.at[a, side],
            toward(0, 1 + 2 * side),
        )

    def core_copy(dx, dz):
        return remote(toks.at[dx, dz, c], toks.at[dx, dz, c], core_s.at[dx, dz], core_r.at[dx, dz], at(dc=1))

    def core_arrival(dx, dz):
        there = toks.at[dx, dz, 1 - c]
        return remote(there, there, core_s.at[dx, dz], core_r.at[dx, dz], at(dc=1))

    def chip(j, q):
        return lut(2 * j + q, CHIP_DX), lut(2 * j + q, CHIP_DZ)

    def service(j):
        for q in range(2):
            dx, dz = chip(j, q)
            a, b = turned(dx, dz)

            @pl.when(b == 2)
            def _():
                pass_on(a, 0).wait_recv()
                pass_on(a, 1).wait_recv()

            @pl.when(lax.rem(b, 2) == 1)
            def _():
                ag_second(a, 4 - b).wait_recv()

            core_copy(dx, dz).start()

    ag_first(1).start()
    ag_first(3).start()
    ag_second(0, 1).start()
    ag_second(0, 3).start()
    for a in (1, 3):
        ag_first(a).wait_recv()
        ag_second(4 - a, 1).start()
        ag_second(4 - a, 3).start()
    ag_first(2).start()
    attn_second(0).wait_send()
    attn_second(1).wait_send()
    service(0)
    for copy in weight_copies():
        copy.wait()

    def y1_copy(j, side):
        n = lax.rem(j, 3)
        return remote(
            pb.at[n, lax.rem(y + 2, 4), pl.ds(side * half_rows, half_rows)],
            y1.at[lax.rem(j, 4), side],
            y1_s.at[n, side],
            y1_r.at[lax.rem(j, 4), side],
            at(dy=1 + 2 * side),
        )

    def y2_copy(j, side):
        n = lax.rem(j, 3)
        return remote(
            pb.at[n, lax.rem(y + 1 + 2 * side, 4)],
            y2.at[lax.rem(j, 4), side],
            y2_s.at[n, side],
            y2_r.at[lax.rem(j, 4), side],
            at(dy=1 + 2 * side),
        )

    def h_copy(j, d):
        spot = hb.at[lax.rem(j, 4), y]
        return remote(spot, spot, h_s.at[lax.rem(j, 4), d - 1], h_r.at[lax.rem(j, 4), d - 1], at(dy=d))

    def h_arrival(j, d):
        spot = hb.at[lax.rem(j, 4), lax.rem(y + 4 - d, 4)]
        return remote(spot, spot, h_s.at[lax.rem(j, 4), d - 1], h_r.at[lax.rem(j, 4), d - 1], at(dy=d))

    def p_copy(j):
        return remote(
            ob.at[lax.rem(j, 2), :, 1 - c],
            pr.at[lax.rem(j, 4)],
            p_s.at[lax.rem(j, 2)],
            p_r.at[lax.rem(j, 4)],
            at(dc=1),
        )

    def first_copy(j, q, outer, inner):
        dev = at(dx=inner * c, dz=inner * (1 - c))
        return remote(cs.at[lax.rem(j, 3), q], fr.at[outer, inner - 1], f_s.at[lax.rem(j, 3), q], f_r.at[outer, inner - 1], dev)

    def second_copy(outer):
        dev = at(dx=outer * (1 - c), dz=outer * c)
        return remote(own.at[outer], sr.at[outer - 1], s_s.at[outer - 1], s_r.at[outer - 1], dev)

    def place(j, q):
        dx, dz = chip(j, q)
        return jnp.where(c == 0, dx, dz), jnp.where(c == 0, dz, dx)

    def project(j):
        chips = [chip(j, q) for q in range(2)]
        core_arrival(*chips[0]).wait_recv()
        core_arrival(*chips[1]).wait_recv()
        picks = []
        for q in range(2):
            for s in range(2):
                m = toks[chips[q][0], chips[q][1], s, :, pl.ds(quarter, META)].astype(F32).T
                codes = m[:top] * cap + m[top : 2 * top]
                pick = jnp.zeros((8 * cap, tokens), F32)
                for k in range(top):
                    pick = jnp.where(rowc[2 * q + s] == codes[k : k + 1, :], 1.0, pick)
                picks.append(pick.astype(BF16))
        picks = [jnp.concatenate(picks[:2], axis=1), jnp.concatenate(picks[2:], axis=1)]

        @pl.loop(0, 2)
        def _(n):
            part = cols(n, quarter // 2)
            value = jnp.zeros((8 * cap, quarter // 2), F32)
            for q in range(2):
                data = toks[chips[q][0], chips[q][1], :, :, part].reshape(2 * tokens, quarter // 2)
                value = value + jnp.dot(picks[q], data, preferred_element_type=F32)
            xb[:, part] = value.astype(BF16)

        for l in range(2):

            @pl.loop(0, 4)
            def _(o):
                pb[lax.rem(j, 3), o, pl.ds(l * half_rows, half_rows), :] = jnp.dot(
                    xb[pl.ds(l * half_rows, half_rows), :], wg[l, o], preferred_element_type=F32
                ).astype(BF16)

        y1_copy(j, 0).start()
        y1_copy(j, 1).start()

    def relay(j):
        n = lax.rem(j, 3)
        for side in range(2):
            y1_copy(j, side).wait()
            o = lax.rem(y + 1 + 2 * side, 4)
            rows = pl.ds(side * half_rows, half_rows)
            value = pb[n, o, rows, :].astype(F32) + y1[lax.rem(j, 4), side].astype(F32)
            pb[n, o, rows, :] = value.astype(BF16)
            y2_copy(j, side).start()

    def activate(j):
        y2_copy(j, 0).wait()
        y2_copy(j, 1).wait()
        slot = lax.rem(j, 4)
        value = pb[lax.rem(j, 3), y].astype(F32) + y2[slot, 0].astype(F32) + y2[slot, 1].astype(F32)
        hb[slot, y] = (jax.nn.silu(value[:, :block]) * value[:, block:]).astype(BF16)
        for d in (1, 3, 2):
            h_copy(j, d).start()

    def expand(j):
        for d in (1, 3, 2):
            h_copy(j, d).wait_send()
            h_arrival(j, d).wait_recv()
        slot = lax.rem(j, 4)
        for l in range(2):
            lhs = jnp.concatenate([hb[slot, o, pl.ds(l * half_rows, half_rows), :] for o in range(4)], axis=1)

            @pl.loop(0, 2)
            def _(n):
                value = jnp.dot(lhs, wd[l, :, cols(n, quarter // 2)], preferred_element_type=F32)
                ob[lax.rem(j, 2), l, :, :, cols(n, quarter // 2)] = value.astype(BF16).reshape(2, 2 * cap, quarter // 2)

        p_copy(j).start()

    def gather_back(j):
        p_copy(j).wait()
        for q in range(2):
            _, inner_before = place(j - 3, q)

            @pl.when((j >= 3) & (inner_before != 0))
            def _():
                first_copy(j, q, 0, 1).wait_send()

        for q in range(2):
            dx, dz = chip(j, q)
            m = toks[dx, dz, c, :, pl.ds(quarter, META)].astype(F32)
            codes, gate = m[:, :top] * cap + m[:, top : 2 * top], m[:, 2 * top : 3 * top]
            sides = []
            for base in (e, e + 1 - 2 * c):
                rows = tab[q : q + 1, :] + (2 * cap * base).astype(F32)
                side = jnp.zeros((tokens, 4 * cap), F32)
                for k in range(top):
                    side = jnp.where(codes[:, k : k + 1] == rows, gate[:, k : k + 1], side)
                sides.append(side.astype(BF16))

            @pl.loop(0, 2)
            def _(n):
                part = cols(n, quarter // 2)
                here = ob[lax.rem(j, 2), :, c, :, part].reshape(4 * cap, quarter // 2)
                other = pr[lax.rem(j, 4), :, :, part].reshape(4 * cap, quarter // 2)
                value = jnp.dot(sides[0], here, preferred_element_type=F32)
                value = value + jnp.dot(sides[1], other, preferred_element_type=F32)
                cs[lax.rem(j, 3), q, :, part] = value.astype(BF16)

            outer, inner = place(j, q)

            @pl.when(inner == 0)
            def _():
                own[outer] = cs[lax.rem(j, 3), q]

            @pl.when(inner != 0)
            def _():
                first_copy(j, q, outer, inner).start()

    def combine(outer):
        value = own[outer].astype(F32)
        for inner in (1, 2, 3):
            first_copy(0, 0, outer, inner).wait_recv()
            value = value + fr[outer, inner - 1].astype(F32)
        return value

    def finish(outer):
        own[outer] = combine(outer).astype(BF16)
        second_copy(outer).start()

    @pl.loop(0, STEPS + 4)
    def _(it):
        @pl.when(it < STEPS)
        def _():
            project(it)

        @pl.when((it >= 1) & (it <= STEPS))
        def _():
            relay(it - 1)

        @pl.when((it >= 2) & (it <= STEPS + 1))
        def _():
            activate(it - 2)

        @pl.when(it == 1)
        def _():
            ag_first(2).wait_recv()
            ag_second(2, 1).start()
            ag_second(2, 3).start()
            pass_on(0, 0).start()
            pass_on(0, 1).start()

        @pl.when(it + 1 < STEPS)
        def _():
            service(it + 1)

        @pl.when(it == 2)
        def _():
            for a in (1, 3):
                pass_on(a, 0).start()
                pass_on(a, 1).start()

        @pl.when(it == 4)
        def _():
            pass_on(2, 0).start()
            pass_on(2, 1).start()

        @pl.when((it >= 3) & (it <= STEPS + 2))
        def _():
            expand(it - 3)

        @pl.when(it >= 4)
        def _():
            gather_back(it - 4)

        @pl.when((c == 1) & (it == 10))
        def _():
            finish(1)
            finish(3)

    @pl.when(c == 0)
    def _():
        finish(1)
        finish(3)

    finish(2)
    value = stream[...].astype(F32) + combine(0)
    for outer in (1, 3, 2):
        second_copy(outer).wait()
        value = value + sr[outer - 1].astype(F32)
    out[...] = value.astype(BF16)

    for side in range(2):
        attn_first(side).wait_send()
    for d in (1, 2, 3):
        ss_copy(d).wait_send()
        ag_first(d).wait_send()
    for a in range(4):
        ag_second(a, 1).wait_send()
        ag_second(a, 3).wait_send()
        pass_on(a, 0).wait_send()
        pass_on(a, 1).wait_send()
        for b in range(4):
            core_copy(a, b).wait_send()
    for j in (STEPS - 3, STEPS - 2, STEPS - 1):
        for q in range(2):
            _, inner = place(j, q)

            @pl.when(inner != 0)
            def _():
                first_copy(j, q, 0, 1).wait_send()


def per_device(attn_partials, residual, norm_gain, gate_up, down, expert_ids, gate_ints):
    tokens, width = residual.shape
    quarter = norm_gain.shape[0]
    local, _, double = gate_up.shape
    hidden = down.shape[1]
    block = hidden // 4
    groups = lax.axis_size("expert")
    top = expert_ids.shape[1]
    cap = 3 * tokens * top // (2 * groups * local)
    rows = 8 * cap
    dma = pltpu.SemaphoreType.DMA
    vmem = pl.BlockSpec(memory_space=pltpu.VMEM)
    anywhere = pl.BlockSpec(memory_space=pl.ANY)
    scratch = [
        pltpu.VMEM((local, 4, quarter, 2 * block), BF16),
        pltpu.VMEM((local, hidden, quarter), BF16),
        pltpu.VMEM((4, 4, 2, tokens, quarter + META), BF16),
        pltpu.VMEM((4, rows, tokens), F32),
        pltpu.VMEM((3, 4, rows, 2 * block), BF16),
        pltpu.VMEM((rows, quarter), BF16),
        pltpu.VMEM((4, 2, rows // 2, 2 * block), BF16),
        pltpu.VMEM((4, 2, rows, 2 * block), BF16),
        pltpu.VMEM((4, 4, rows, block), BF16),
        pltpu.VMEM((2, local, 2, 2 * cap, quarter), BF16),
        pltpu.VMEM((4, local, 2 * cap, quarter), BF16),
        pltpu.VMEM((4, tokens, quarter), BF16),
        pltpu.VMEM((3, 2, tokens, quarter), BF16),
        pltpu.VMEM((4, 3, tokens, quarter), BF16),
        pltpu.VMEM((3, tokens, quarter), BF16),
        pltpu.VMEM((tokens, quarter), BF16),
        pltpu.VMEM((4, tokens, META), F32),
        dma((18,)),
        dma((4,)),
        dma((2,)),
        dma((2,)),
        dma((2,)),
        dma((2,)),
        dma((3,)),
        dma((3,)),
        dma((4,)),
        dma((4,)),
        dma((4, 4)),
        dma((4, 4)),
        dma((4, 2)),
        dma((4, 2)),
        dma((4, 4)),
        dma((4, 4)),
        dma((3, 2)),
        dma((4, 2)),
        dma((3, 2)),
        dma((4, 2)),
        dma((4, 3)),
        dma((4, 3)),
        dma((2,)),
        dma((4,)),
        dma((3, 2)),
        dma((4, 3)),
        dma((3,)),
        dma((3,)),
    ]
    return pl.pallas_call(
        functools.partial(layer_kernel, cap, groups * local),
        out_shape=jax.ShapeDtypeStruct((tokens, quarter), BF16),
        in_specs=[anywhere, anywhere, vmem, anywhere, anywhere, vmem, vmem, vmem],
        out_specs=vmem,
        scratch_shapes=scratch,
        compiler_params=pltpu.CompilerParams(collective_id=0, has_side_effects=True, vmem_limit_bytes=62 * 2**20),
        cost_estimate=pl.CostEstimate(flops=30 * 10**9, bytes_accessed=30 * 10**6, transcendentals=0),
    )(
        attn_partials[0],
        residual,
        norm_gain,
        gate_up,
        down,
        expert_ids.T,
        gate_ints.T,
        jnp.asarray(row_table(cap)),
    )


def solution(mesh):
    in_specs = (
        P("tensor", "expert", None),
        P("expert", None),
        P("tensor"),
        P("expert", "tensor", None),
        P("expert", None, "tensor"),
        P("expert", None),
        P("expert", None),
    )
    return jax.shard_map(
        per_device, mesh=mesh, in_specs=in_specs, out_specs=P("expert", "tensor"), check_vma=False
    )
```

```python
import functools
import jax
import jax.numpy as jnp
import numpy as np
from jax import lax
from jax.experimental import pallas as pl
from jax.experimental.pallas import tpu as pltpu
from jax.sharding import PartitionSpec as P

MESH = pl.DeviceIdType.MESH
F32, BF16 = jnp.float32, jnp.bfloat16
CHIP_DX = (0, 0, 1, 3, 1, 3, 1, 3, 1, 3, 2, 2, 2, 2, 0, 0)
CHIP_DZ = (1, 3, 0, 0, 1, 3, 3, 1, 2, 2, 1, 3, 2, 0, 2, 0)
STEPS = 8
META = 128


def lut(index, values):
    result = jnp.int32(values[0])
    for at, value in enumerate(values):
        if at:
            result = jnp.where(index == at, jnp.int32(value), result)
    return result


def row_table(cap):
    table = np.full((8, 4 * cap), -1e6, np.float32)
    for l in range(2):
        for q in range(2):
            for j in range(cap):
                table[q, (l * 2 + q) * cap + j] = l * cap + j
    return table


def layer_kernel(
    cap,
    experts_all,
    attn,
    resid,
    gain,
    wgu,
    wdn,
    ids,
    ints,
    tab,
    out,
    wg,
    wd,
    toks,
    rowc,
    pb,
    xb,
    y1,
    y2,
    hb,
    ob,
    pr,
    own,
    cs,
    fr,
    sr,
    stream,
    ssb,
    w_sem,
    l_sem,
    a1_s,
    a1_r,
    a2_s,
    a2_r,
    ss_s,
    ss_r,
    ag1_s,
    ag1_r,
    ag2_s,
    ag2_r,
    agf_s,
    agf_r,
    core_s,
    core_r,
    y1_s,
    y1_r,
    y2_s,
    y2_r,
    h_s,
    h_r,
    p_s,
    p_r,
    f_s,
    f_r,
    s_s,
    s_r,
):
    e = lax.axis_index("expert")
    y = lax.axis_index("tensor")
    x, z, c = e // 8, lax.rem(e // 2, 4), lax.rem(e, 2)
    tokens, quarter = stream.shape
    top = ids.shape[0]
    width = 4 * quarter
    half_rows = 4 * cap
    block = hb.shape[3]

    def at(dx=0, dz=0, dc=0, dy=0):
        ex = (lax.rem(x + dx, 4) * 4 + lax.rem(z + dz, 4)) * 2 + lax.rem(c + dc, 2)
        return (ex, lax.rem(y + dy, 4))

    def remote(src, dst, ssem, rsem, dev):
        return pltpu.make_async_remote_copy(
            src_ref=src, dst_ref=dst, send_sem=ssem, recv_sem=rsem, device_id=dev, device_id_type=MESH
        )

    def cols(start, size):
        return pl.ds(pl.multiple_of(start * size, size), size)

    barrier = pltpu.get_barrier_semaphore()
    peers = [at(dy=d) for d in (1, 2, 3)] + [at(dx=d) for d in (1, 2, 3)] + [at(dz=d) for d in (1, 2, 3)] + [at(dc=1)]
    for peer in peers:
        pl.semaphore_signal(barrier, inc=1, device_id=peer, device_id_type=MESH)
    pl.semaphore_wait(barrier, len(peers))

    half = tokens // 2

    def attn_first(side):
        rows = pl.ds(side * half, half)
        source = attn.at[rows, cols(lax.rem(y + 2, 4), quarter)]
        return remote(source, fr.at[1, 2, rows], a1_s.at[side], a1_r.at[side], at(dy=1 + 2 * side))

    def attn_second(side):
        return remote(cs.at[1, side], fr.at[1, side], a2_s.at[side], a2_r.at[side], at(dy=1 + 2 * side))

    attn_first(0).start()
    attn_first(1).start()
    beside = [
        pltpu.make_async_copy(attn.at[:, cols(lax.rem(y + 1 + 2 * side, 4), quarter)], cs.at[1, side], l_sem.at[side])
        for side in range(2)
    ]
    mine = pltpu.make_async_copy(attn.at[:, cols(y, quarter)], cs.at[0, 0], l_sem.at[2])
    rest = pltpu.make_async_copy(resid.at[:, cols(y, quarter)], cs.at[0, 1], l_sem.at[3])
    for copy in (*beside, mine, rest):
        copy.start()

    def weight_copies():
        copies = []
        for l in range(2):
            for o in range(4):
                for g in range(2):
                    copies.append(
                        pltpu.make_async_copy(
                            wgu.at[l, :, pl.ds(g * 4 * block + o * block, block)],
                            wg.at[l, o, :, pl.ds(g * block, block)],
                            w_sem.at[(l * 4 + o) * 2 + g],
                        )
                    )
            copies.append(pltpu.make_async_copy(wdn.at[l], wd.at[l], w_sem.at[16 + l]))
        return copies

    for copy in weight_copies():
        copy.start()
    for side in range(2):
        rows = pl.ds(side * half, half)
        beside[side].wait()
        attn_first(side).wait_recv()
        value = cs[1, side, rows, :].astype(F32) + fr[1, 2, rows, :].astype(F32)
        cs[1, side, rows, :] = value.astype(BF16)
        attn_second(side).start()

    experts = lax.broadcasted_iota(jnp.int32, (experts_all, tokens), 0)
    pick_row = lax.broadcasted_iota(jnp.int32, (top, tokens), 0)
    id_block = ids[...]
    hits = jnp.zeros((experts_all, tokens), F32)
    for k in range(top):
        hits = hits + jnp.where(id_block[k : k + 1, :] == experts, 1.0, 0.0)
    earlier = lax.broadcasted_iota(jnp.int32, (tokens, tokens), 0) < lax.broadcasted_iota(jnp.int32, (tokens, tokens), 1)
    count = jnp.dot(hits.astype(BF16), jnp.where(earlier, 1.0, 0.0).astype(BF16), preferred_element_type=F32)
    slots = jnp.zeros((top, tokens), F32)
    for k in range(top):
        slot = jnp.sum(jnp.where(id_block[k : k + 1, :] == experts, count, 0.0), axis=0, keepdims=True)
        slots = jnp.where(pick_row == k, slot, slots)
    gate_float = ints[...].astype(F32)
    gates = 2.5 * gate_float / jnp.sum(gate_float, axis=0, keepdims=True)
    rest_rows = jnp.zeros((META - 3 * top, tokens), F32)
    meta = jnp.concatenate([id_block.astype(F32), slots, gates, rest_rows], axis=0)
    toks[0, 0, c, :, pl.ds(quarter, META)] = meta.T.astype(BF16)

    r = lax.broadcasted_iota(jnp.int32, (8 * cap, tokens), 0)
    l_of = (r >= 4 * cap).astype(jnp.int32)
    r = r - 4 * cap * l_of
    s_of = (r >= 2 * cap).astype(jnp.int32)
    r = r - 2 * cap * s_of
    q_of = (r >= cap).astype(jnp.int32)
    code = (r - cap * q_of + cap * l_of + 2 * cap * e).astype(F32)
    for q in range(2):
        for s in range(2):
            rowc[2 * q + s] = jnp.where((q_of == q) & (s_of == s), code, -1e6)

    mine.wait()
    rest.wait()
    attn_second(0).wait_recv()
    attn_second(1).wait_recv()
    attention = cs[0, 0].astype(F32) + fr[1, 0].astype(F32) + fr[1, 1].astype(F32)
    summed = (cs[0, 1].astype(F32) + attention).astype(BF16)
    stream[...] = summed
    wide = summed.astype(F32)
    ssb[0] = jnp.broadcast_to(jnp.sum(wide * wide, axis=1, keepdims=True), (tokens, META))

    def ss_copy(d):
        return remote(ssb.at[0], ssb.at[d], ss_s.at[d - 1], ss_r.at[d - 1], at(dy=d))

    for d in (1, 3, 2):
        ss_copy(d).start()
    for d in (1, 3, 2):
        ss_copy(d).wait_recv()
    total = (ssb[0] + ssb[1] + ssb[2] + ssb[3])[:, :1]
    wide = stream[...].astype(F32)
    normed = wide * lax.rsqrt(total / width + 1e-06) * gain[...].reshape(1, quarter)
    toks[0, 0, c, :, pl.ds(0, quarter)] = normed.astype(BF16)

    def turned(a, b):
        return a * c + b * (1 - c), a * (1 - c) + b * c

    def spot(a, b):
        dx, dz = turned(a, b)
        return toks.at[dx, dz, c]

    def toward(a, b):
        dx, dz = turned(a, b)
        return at(dx=dx, dz=dz)

    def ag_first(a):
        return remote(spot(0, 0), spot(4 - a, 0), ag1_s.at[a], ag1_r.at[4 - a], toward(a, 0))

    def ag_second(a, b):
        return remote(spot(a, 0), spot(a, 4 - b), ag2_s.at[a, b], ag2_r.at[a, 4 - b], toward(0, b))

    def pass_on(a, side):
        rows = pl.ds(side * half, half)
        return remote(
            spot(a, 3 - 2 * side).at[rows],
            spot(a, 2).at[rows],
            agf_s.at[a, side],
            agf_r.at[a, side],
            toward(0, 1 + 2 * side),
        )

    def core_copy(dx, dz):
        return remote(toks.at[dx, dz, c], toks.at[dx, dz, c], core_s.at[dx, dz], core_r.at[dx, dz], at(dc=1))

    def core_arrival(dx, dz):
        there = toks.at[dx, dz, 1 - c]
        return remote(there, there, core_s.at[dx, dz], core_r.at[dx, dz], at(dc=1))

    def chip(j, q):
        return lut(2 * j + q, CHIP_DX), lut(2 * j + q, CHIP_DZ)

    def service(j):
        for q in range(2):
            dx, dz = chip(j, q)
            a, b = turned(dx, dz)

            @pl.when(b == 2)
            def _():
                pass_on(a, 0).wait_recv()
                pass_on(a, 1).wait_recv()

            @pl.when((lax.rem(b, 2) == 1) & (a != 0))
            def _():
                ag_second(a, 4 - b).wait_recv()

            core_copy(dx, dz).start()

    ag_first(1).start()
    ag_first(3).start()
    ag_second(0, 1).start()
    ag_second(0, 3).start()
    for a in (1, 3):
        ag_first(a).wait_recv()
        ag_second(0, a).wait_recv()
    attn_second(0).wait_send()
    attn_second(1).wait_send()
    service(0)
    service(1)
    for a in (1, 3):
        ag_second(a, 1).start()
        ag_second(a, 3).start()
    ag_first(2).start()
    for copy in weight_copies():
        copy.wait()

    def y1_copy(j, side):
        n = lax.rem(j, 3)
        return remote(
            pb.at[n, lax.rem(y + 2, 4), pl.ds(side * half_rows, half_rows)],
            y1.at[lax.rem(j, 4), side],
            y1_s.at[n, side],
            y1_r.at[lax.rem(j, 4), side],
            at(dy=1 + 2 * side),
        )

    def y2_copy(j, side):
        n = lax.rem(j, 3)
        return remote(
            pb.at[n, lax.rem(y + 1 + 2 * side, 4)],
            y2.at[lax.rem(j, 4), side],
            y2_s.at[n, side],
            y2_r.at[lax.rem(j, 4), side],
            at(dy=1 + 2 * side),
        )

    def h_copy(j, d):
        spot = hb.at[lax.rem(j, 4), y]
        return remote(spot, spot, h_s.at[lax.rem(j, 4), d - 1], h_r.at[lax.rem(j, 4), d - 1], at(dy=d))

    def h_arrival(j, d):
        spot = hb.at[lax.rem(j, 4), lax.rem(y + 4 - d, 4)]
        return remote(spot, spot, h_s.at[lax.rem(j, 4), d - 1], h_r.at[lax.rem(j, 4), d - 1], at(dy=d))

    def p_copy(j):
        return remote(
            ob.at[lax.rem(j, 2), :, 1 - c],
            pr.at[lax.rem(j, 4)],
            p_s.at[lax.rem(j, 2)],
            p_r.at[lax.rem(j, 4)],
            at(dc=1),
        )

    def first_copy(j, q, outer, inner):
        dev = at(dx=inner * c, dz=inner * (1 - c))
        return remote(cs.at[lax.rem(j, 3), q], fr.at[outer, inner - 1], f_s.at[lax.rem(j, 3), q], f_r.at[outer, inner - 1], dev)

    def second_copy(outer):
        dev = at(dx=outer * (1 - c), dz=outer * c)
        return remote(own.at[outer], sr.at[outer - 1], s_s.at[outer - 1], s_r.at[outer - 1], dev)

    def place(j, q):
        dx, dz = chip(j, q)
        return jnp.where(c == 0, dx, dz), jnp.where(c == 0, dz, dx)

    def project(j):
        chips = [chip(j, q) for q in range(2)]
        core_arrival(*chips[0]).wait_recv()
        core_arrival(*chips[1]).wait_recv()
        picks = []
        for q in range(2):
            for s in range(2):
                m = toks[chips[q][0], chips[q][1], s, :, pl.ds(quarter, META)].astype(F32).T
                codes = m[:top] * cap + m[top : 2 * top]
                pick = jnp.zeros((8 * cap, tokens), F32)
                for k in range(top):
                    pick = jnp.where(rowc[2 * q + s] == codes[k : k + 1, :], 1.0, pick)
                picks.append(pick.astype(BF16))
        picks = [jnp.concatenate(picks[:2], axis=1), jnp.concatenate(picks[2:], axis=1)]

        @pl.loop(0, 2)
        def _(n):
            part = cols(n, quarter // 2)
            value = jnp.zeros((8 * cap, quarter // 2), F32)
            for q in range(2):
                data = toks[chips[q][0], chips[q][1], :, :, part].reshape(2 * tokens, quarter // 2)
                value = value + jnp.dot(picks[q], data, preferred_element_type=F32)
            xb[:, part] = value.astype(BF16)

        for l in range(2):

            @pl.loop(0, 4)
            def _(o):
                pb[lax.rem(j, 3), o, pl.ds(l * half_rows, half_rows), :] = jnp.dot(
                    xb[pl.ds(l * half_rows, half_rows), :], wg[l, o], preferred_element_type=F32
                ).astype(BF16)

        y1_copy(j, 0).start()
        y1_copy(j, 1).start()

    def relay(j):
        n = lax.rem(j, 3)
        for side in range(2):
            y1_copy(j, side).wait()
            o = lax.rem(y + 1 + 2 * side, 4)
            rows = pl.ds(side * half_rows, half_rows)
            value = pb[n, o, rows, :].astype(F32) + y1[lax.rem(j, 4), side].astype(F32)
            pb[n, o, rows, :] = value.astype(BF16)
            y2_copy(j, side).start()

    def activate(j):
        y2_copy(j, 0).wait()
        y2_copy(j, 1).wait()
        slot = lax.rem(j, 4)
        value = pb[lax.rem(j, 3), y].astype(F32) + y2[slot, 0].astype(F32) + y2[slot, 1].astype(F32)
        hb[slot, y] = (jax.nn.silu(value[:, :block]) * value[:, block:]).astype(BF16)
        for d in (1, 3, 2):
            h_copy(j, d).start()

    def expand(j):
        for d in (1, 3, 2):
            h_copy(j, d).wait_send()
            h_arrival(j, d).wait_recv()
        slot = lax.rem(j, 4)
        for l in range(2):
            lhs = jnp.concatenate([hb[slot, o, pl.ds(l * half_rows, half_rows), :] for o in range(4)], axis=1)

            @pl.loop(0, 2)
            def _(n):
                value = jnp.dot(lhs, wd[l, :, cols(n, quarter // 2)], preferred_element_type=F32)
                ob[lax.rem(j, 2), l, :, :, cols(n, quarter // 2)] = value.astype(BF16).reshape(2, 2 * cap, quarter // 2)

        p_copy(j).start()

    def gather_back(j):
        p_copy(j).wait()
        for q in range(2):
            _, inner_before = place(j - 3, q)

            @pl.when((j >= 3) & (inner_before != 0))
            def _():
                first_copy(j, q, 0, 1).wait_send()

        for q in range(2):
            dx, dz = chip(j, q)
            m = toks[dx, dz, c, :, pl.ds(quarter, META)].astype(F32)
            codes, gate = m[:, :top] * cap + m[:, top : 2 * top], m[:, 2 * top : 3 * top]
            sides = []
            for base in (e, e + 1 - 2 * c):
                rows = tab[q : q + 1, :] + (2 * cap * base).astype(F32)
                side = jnp.zeros((tokens, 4 * cap), F32)
                for k in range(top):
                    side = jnp.where(codes[:, k : k + 1] == rows, gate[:, k : k + 1], side)
                sides.append(side.astype(BF16))

            @pl.loop(0, 2)
            def _(n):
                part = cols(n, quarter // 2)
                here = ob[lax.rem(j, 2), :, c, :, part].reshape(4 * cap, quarter // 2)
                other = pr[lax.rem(j, 4), :, :, part].reshape(4 * cap, quarter // 2)
                value = jnp.dot(sides[0], here, preferred_element_type=F32)
                value = value + jnp.dot(sides[1], other, preferred_element_type=F32)
                cs[lax.rem(j, 3), q, :, part] = value.astype(BF16)

            outer, inner = place(j, q)

            @pl.when(inner == 0)
            def _():
                own[outer] = cs[lax.rem(j, 3), q]

            @pl.when(inner != 0)
            def _():
                first_copy(j, q, outer, inner).start()

    def combine(outer):
        value = own[outer].astype(F32)
        for inner in (1, 2, 3):
            first_copy(0, 0, outer, inner).wait_recv()
            value = value + fr[outer, inner - 1].astype(F32)
        return value

    def finish(outer):
        own[outer] = combine(outer).astype(BF16)
        second_copy(outer).start()

    @pl.loop(0, STEPS + 4)
    def _(it):
        @pl.when(it < STEPS)
        def _():
            project(it)

        @pl.when((it >= 1) & (it <= STEPS))
        def _():
            relay(it - 1)

        @pl.when((it >= 3) & (it <= STEPS + 1))
        def _():
            activate(it - 2)

        @pl.when(it == 1)
        def _():
            ag_first(2).wait_recv()
            ag_second(2, 1).start()
            ag_second(2, 3).start()
            pass_on(0, 0).start()
            pass_on(0, 1).start()

        @pl.when((it >= 1) & (it + 1 < STEPS))
        def _():
            service(it + 1)

        @pl.when(it == 1)
        def _():
            activate(0)

        @pl.when(it == 2)
        def _():
            for a in (1, 3):
                pass_on(a, 0).start()
                pass_on(a, 1).start()

        @pl.when(it == 4)
        def _():
            pass_on(2, 0).start()
            pass_on(2, 1).start()

        @pl.when((it >= 3) & (it <= STEPS + 2))
        def _():
            expand(it - 3)

        @pl.when(it >= 4)
        def _():
            gather_back(it - 4)

        @pl.when((c == 0) & (it == 10))
        def _():
            finish(1)
            finish(3)

    @pl.when(c == 1)
    def _():
        finish(1)
        finish(3)

    finish(2)
    value = stream[...].astype(F32) + combine(0)
    for outer in (1, 3, 2):
        second_copy(outer).wait()
        value = value + sr[outer - 1].astype(F32)
    out[...] = value.astype(BF16)

    for side in range(2):
        attn_first(side).wait_send()
    for d in (1, 2, 3):
        ss_copy(d).wait_send()
        ag_first(d).wait_send()
    for a in range(4):
        ag_second(a, 1).wait_send()
        ag_second(a, 3).wait_send()
        pass_on(a, 0).wait_send()
        pass_on(a, 1).wait_send()
        for b in range(4):
            core_copy(a, b).wait_send()
    for j in (STEPS - 3, STEPS - 2, STEPS - 1):
        for q in range(2):
            _, inner = place(j, q)

            @pl.when(inner != 0)
            def _():
                first_copy(j, q, 0, 1).wait_send()


def per_device(attn_partials, residual, norm_gain, gate_up, down, expert_ids, gate_ints):
    tokens, width = residual.shape
    quarter = norm_gain.shape[0]
    local, _, double = gate_up.shape
    hidden = down.shape[1]
    block = hidden // 4
    groups = lax.axis_size("expert")
    top = expert_ids.shape[1]
    cap = 3 * tokens * top // (2 * groups * local)
    rows = 8 * cap
    dma = pltpu.SemaphoreType.DMA
    vmem = pl.BlockSpec(memory_space=pltpu.VMEM)
    anywhere = pl.BlockSpec(memory_space=pl.ANY)
    scratch = [
        pltpu.VMEM((local, 4, quarter, 2 * block), BF16),
        pltpu.VMEM((local, hidden, quarter), BF16),
        pltpu.VMEM((4, 4, 2, tokens, quarter + META), BF16),
        pltpu.VMEM((4, rows, tokens), F32),
        pltpu.VMEM((3, 4, rows, 2 * block), BF16),
        pltpu.VMEM((rows, quarter), BF16),
        pltpu.VMEM((4, 2, rows // 2, 2 * block), BF16),
        pltpu.VMEM((4, 2, rows, 2 * block), BF16),
        pltpu.VMEM((4, 4, rows, block), BF16),
        pltpu.VMEM((2, local, 2, 2 * cap, quarter), BF16),
        pltpu.VMEM((4, local, 2 * cap, quarter), BF16),
        pltpu.VMEM((4, tokens, quarter), BF16),
        pltpu.VMEM((3, 2, tokens, quarter), BF16),
        pltpu.VMEM((4, 3, tokens, quarter), BF16),
        pltpu.VMEM((3, tokens, quarter), BF16),
        pltpu.VMEM((tokens, quarter), BF16),
        pltpu.VMEM((4, tokens, META), F32),
        dma((18,)),
        dma((4,)),
        dma((2,)),
        dma((2,)),
        dma((2,)),
        dma((2,)),
        dma((3,)),
        dma((3,)),
        dma((4,)),
        dma((4,)),
        dma((4, 4)),
        dma((4, 4)),
        dma((4, 2)),
        dma((4, 2)),
        dma((4, 4)),
        dma((4, 4)),
        dma((3, 2)),
        dma((4, 2)),
        dma((3, 2)),
        dma((4, 2)),
        dma((4, 3)),
        dma((4, 3)),
        dma((2,)),
        dma((4,)),
        dma((3, 2)),
        dma((4, 3)),
        dma((3,)),
        dma((3,)),
    ]
    return pl.pallas_call(
        functools.partial(layer_kernel, cap, groups * local),
        out_shape=jax.ShapeDtypeStruct((tokens, quarter), BF16),
        in_specs=[anywhere, anywhere, vmem, anywhere, anywhere, vmem, vmem, vmem],
        out_specs=vmem,
        scratch_shapes=scratch,
        compiler_params=pltpu.CompilerParams(collective_id=0, has_side_effects=True, vmem_limit_bytes=62 * 2**20),
        cost_estimate=pl.CostEstimate(flops=30 * 10**9, bytes_accessed=30 * 10**6, transcendentals=0),
    )(
        attn_partials[0],
        residual,
        norm_gain,
        gate_up,
        down,
        expert_ids.T,
        gate_ints.T,
        jnp.asarray(row_table(cap)),
    )


def solution(mesh):
    in_specs = (
        P("tensor", "expert", None),
        P("expert", None),
        P("tensor"),
        P("expert", "tensor", None),
        P("expert", None, "tensor"),
        P("expert", None),
        P("expert", None),
    )
    return jax.shard_map(
        per_device, mesh=mesh, in_specs=in_specs, out_specs=P("expert", "tensor"), check_vma=False
    )
```

```python
import functools
import jax
import jax.numpy as jnp
import numpy as np
from jax import lax
from jax.experimental import pallas as pl
from jax.experimental.pallas import tpu as pltpu
from jax.sharding import PartitionSpec as P

MESH = pl.DeviceIdType.MESH
F32, BF16 = jnp.float32, jnp.bfloat16
CHIP_DX = (0, 0, 1, 3, 1, 3, 1, 3, 1, 3, 2, 2, 2, 2, 0, 0)
CHIP_DZ = (1, 3, 0, 0, 1, 3, 3, 1, 2, 2, 1, 3, 2, 0, 2, 0)
STEPS = 8
META = 128


def lut(index, values):
    result = jnp.int32(values[0])
    for at, value in enumerate(values):
        if at:
            result = jnp.where(index == at, jnp.int32(value), result)
    return result


def row_table(cap):
    table = np.full((8, 4 * cap), -1e6, np.float32)
    for l in range(2):
        for q in range(2):
            for j in range(cap):
                table[q, (l * 2 + q) * cap + j] = l * cap + j
    return table


def layer_kernel(
    cap,
    experts_all,
    attn,
    resid,
    gain,
    wgu,
    wdn,
    ids,
    ints,
    tab,
    out,
    wg,
    wd,
    toks,
    rowc,
    pb,
    xb,
    y1,
    y2,
    hb,
    ob,
    pr,
    own,
    cs,
    fr,
    sr,
    stream,
    ssb,
    w_sem,
    l_sem,
    a1_s,
    a1_r,
    a2_s,
    a2_r,
    ss_s,
    ss_r,
    ag1_s,
    ag1_r,
    ag2_s,
    ag2_r,
    agf_s,
    agf_r,
    core_s,
    core_r,
    y1_s,
    y1_r,
    y2_s,
    y2_r,
    h_s,
    h_r,
    p_s,
    p_r,
    f_s,
    f_r,
    s_s,
    s_r,
):
    e = lax.axis_index("expert")
    y = lax.axis_index("tensor")
    x, z, c = e // 8, lax.rem(e // 2, 4), lax.rem(e, 2)
    tokens, quarter = stream.shape
    top = ids.shape[0]
    width = 4 * quarter
    half_rows = 4 * cap
    block = hb.shape[3]

    def at(dx=0, dz=0, dc=0, dy=0):
        ex = (lax.rem(x + dx, 4) * 4 + lax.rem(z + dz, 4)) * 2 + lax.rem(c + dc, 2)
        return (ex, lax.rem(y + dy, 4))

    def remote(src, dst, ssem, rsem, dev):
        return pltpu.make_async_remote_copy(
            src_ref=src, dst_ref=dst, send_sem=ssem, recv_sem=rsem, device_id=dev, device_id_type=MESH
        )

    def cols(start, size):
        return pl.ds(pl.multiple_of(start * size, size), size)

    barrier = pltpu.get_barrier_semaphore()
    peers = [at(dy=d) for d in (1, 2, 3)] + [at(dx=d) for d in (1, 2, 3)] + [at(dz=d) for d in (1, 2, 3)] + [at(dc=1)]
    for peer in peers:
        pl.semaphore_signal(barrier, inc=1, device_id=peer, device_id_type=MESH)
    pl.semaphore_wait(barrier, len(peers))

    half = tokens // 2

    def attn_first(side):
        rows = pl.ds(side * half, half)
        source = attn.at[rows, cols(lax.rem(y + 2, 4), quarter)]
        return remote(source, fr.at[1, 2, rows], a1_s.at[side], a1_r.at[side], at(dy=1 + 2 * side))

    def attn_second(side):
        return remote(cs.at[1, side], fr.at[1, side], a2_s.at[side], a2_r.at[side], at(dy=1 + 2 * side))

    attn_first(0).start()
    attn_first(1).start()
    beside = [
        pltpu.make_async_copy(attn.at[:, cols(lax.rem(y + 1 + 2 * side, 4), quarter)], cs.at[1, side], l_sem.at[side])
        for side in range(2)
    ]
    mine = pltpu.make_async_copy(attn.at[:, cols(y, quarter)], cs.at[0, 0], l_sem.at[2])
    rest = pltpu.make_async_copy(resid.at[:, cols(y, quarter)], cs.at[0, 1], l_sem.at[3])
    for copy in (*beside, mine, rest):
        copy.start()

    def weight_copies():
        copies = []
        for l in range(2):
            for o in range(4):
                for g in range(2):
                    copies.append(
                        pltpu.make_async_copy(
                            wgu.at[l, :, pl.ds(g * 4 * block + o * block, block)],
                            wg.at[l, o, :, pl.ds(g * block, block)],
                            w_sem.at[(l * 4 + o) * 2 + g],
                        )
                    )
            copies.append(pltpu.make_async_copy(wdn.at[l], wd.at[l], w_sem.at[16 + l]))
        return copies

    for copy in weight_copies():
        copy.start()
    for side in range(2):
        rows = pl.ds(side * half, half)
        beside[side].wait()
        attn_first(side).wait_recv()
        value = cs[1, side, rows, :].astype(F32) + fr[1, 2, rows, :].astype(F32)
        cs[1, side, rows, :] = value.astype(BF16)
        attn_second(side).start()

    experts = lax.broadcasted_iota(jnp.int32, (experts_all, tokens), 0)
    pick_row = lax.broadcasted_iota(jnp.int32, (top, tokens), 0)
    id_block = ids[...]
    hits = jnp.zeros((experts_all, tokens), F32)
    for k in range(top):
        hits = hits + jnp.where(id_block[k : k + 1, :] == experts, 1.0, 0.0)
    earlier = lax.broadcasted_iota(jnp.int32, (tokens, tokens), 0) < lax.broadcasted_iota(jnp.int32, (tokens, tokens), 1)
    count = jnp.dot(hits.astype(BF16), jnp.where(earlier, 1.0, 0.0).astype(BF16), preferred_element_type=F32)
    slots = jnp.zeros((top, tokens), F32)
    for k in range(top):
        slot = jnp.sum(jnp.where(id_block[k : k + 1, :] == experts, count, 0.0), axis=0, keepdims=True)
        slots = jnp.where(pick_row == k, slot, slots)
    gate_float = ints[...].astype(F32)
    gates = 2.5 * gate_float / jnp.sum(gate_float, axis=0, keepdims=True)
    rest_rows = jnp.zeros((META - 3 * top, tokens), F32)
    meta = jnp.concatenate([id_block.astype(F32), slots, gates, rest_rows], axis=0)
    toks[0, 0, c, :, pl.ds(quarter, META)] = meta.T.astype(BF16)

    r = lax.broadcasted_iota(jnp.int32, (8 * cap, tokens), 0)
    l_of = (r >= 4 * cap).astype(jnp.int32)
    r = r - 4 * cap * l_of
    s_of = (r >= 2 * cap).astype(jnp.int32)
    r = r - 2 * cap * s_of
    q_of = (r >= cap).astype(jnp.int32)
    code = (r - cap * q_of + cap * l_of + 2 * cap * e).astype(F32)
    for q in range(2):
        for s in range(2):
            rowc[2 * q + s] = jnp.where((q_of == q) & (s_of == s), code, -1e6)

    mine.wait()
    rest.wait()
    attn_second(0).wait_recv()
    attn_second(1).wait_recv()
    attention = cs[0, 0].astype(F32) + fr[1, 0].astype(F32) + fr[1, 1].astype(F32)
    summed = (cs[0, 1].astype(F32) + attention).astype(BF16)
    stream[...] = summed
    wide = summed.astype(F32)
    squares = jnp.sum(wide * wide, axis=1, keepdims=True)
    ssb[0] = jnp.broadcast_to(squares, (tokens, META)).T[:8]

    def ss_copy(d):
        return remote(ssb.at[0], ssb.at[d], ss_s.at[d - 1], ss_r.at[d - 1], at(dy=d))

    for d in (1, 3, 2):
        ss_copy(d).start()
    for d in (1, 3, 2):
        ss_copy(d).wait_recv()
    total = ssb[0] + ssb[1] + ssb[2] + ssb[3]
    total = jnp.broadcast_to(total[:1], (META, tokens)).T[:, :1]
    wide = stream[...].astype(F32)
    normed = wide * lax.rsqrt(total / width + 1e-06) * gain[...].reshape(1, quarter)
    toks[0, 0, c, :, pl.ds(0, quarter)] = normed.astype(BF16)

    def turned(a, b):
        return a * c + b * (1 - c), a * (1 - c) + b * c

    def spot(a, b):
        dx, dz = turned(a, b)
        return toks.at[dx, dz, c]

    def toward(a, b):
        dx, dz = turned(a, b)
        return at(dx=dx, dz=dz)

    def ag_first(a):
        return remote(spot(0, 0), spot(4 - a, 0), ag1_s.at[a], ag1_r.at[4 - a], toward(a, 0))

    def ag_second(a, b):
        return remote(spot(a, 0), spot(a, 4 - b), ag2_s.at[a, b], ag2_r.at[a, 4 - b], toward(0, b))

    def pass_on(a, side):
        rows = pl.ds(side * half, half)
        return remote(
            spot(a, 3 - 2 * side).at[rows],
            spot(a, 2).at[rows],
            agf_s.at[a, side],
            agf_r.at[a, side],
            toward(0, 1 + 2 * side),
        )

    def core_copy(dx, dz):
        return remote(toks.at[dx, dz, c], toks.at[dx, dz, c], core_s.at[dx, dz], core_r.at[dx, dz], at(dc=1))

    def core_arrival(dx, dz):
        there = toks.at[dx, dz, 1 - c]
        return remote(there, there, core_s.at[dx, dz], core_r.at[dx, dz], at(dc=1))

    def chip(j, q):
        return lut(2 * j + q, CHIP_DX), lut(2 * j + q, CHIP_DZ)

    def service(j):
        for q in range(2):
            dx, dz = chip(j, q)
            a, b = turned(dx, dz)

            @pl.when(b == 2)
            def _():
                pass_on(a, 0).wait_recv()
                pass_on(a, 1).wait_recv()

            @pl.when((lax.rem(b, 2) == 1) & (a != 0))
            def _():
                ag_second(a, 4 - b).wait_recv()

            core_copy(dx, dz).start()

    ag_first(1).start()
    ag_first(3).start()
    ag_second(0, 1).start()
    ag_second(0, 3).start()
    for a in (1, 3):
        ag_first(a).wait_recv()
        ag_second(0, a).wait_recv()
    attn_second(0).wait_send()
    attn_second(1).wait_send()
    service(0)
    service(1)
    for a in (1, 3):
        ag_second(a, 1).start()
        ag_second(a, 3).start()
    ag_first(2).start()
    for copy in weight_copies():
        copy.wait()

    def y1_copy(j, side):
        n = lax.rem(j, 3)
        return remote(
            pb.at[n, lax.rem(y + 2, 4), pl.ds(side * half_rows, half_rows)],
            y1.at[lax.rem(j, 4), side],
            y1_s.at[n, side],
            y1_r.at[lax.rem(j, 4), side],
            at(dy=1 + 2 * side),
        )

    def y2_copy(j, side):
        n = lax.rem(j, 3)
        return remote(
            pb.at[n, lax.rem(y + 1 + 2 * side, 4)],
            y2.at[lax.rem(j, 4), side],
            y2_s.at[n, side],
            y2_r.at[lax.rem(j, 4), side],
            at(dy=1 + 2 * side),
        )

    def h_copy(j, d):
        spot = hb.at[lax.rem(j, 4), y]
        return remote(spot, spot, h_s.at[lax.rem(j, 4), d - 1], h_r.at[lax.rem(j, 4), d - 1], at(dy=d))

    def h_arrival(j, d):
        spot = hb.at[lax.rem(j, 4), lax.rem(y + 4 - d, 4)]
        return remote(spot, spot, h_s.at[lax.rem(j, 4), d - 1], h_r.at[lax.rem(j, 4), d - 1], at(dy=d))

    def p_copy(j):
        return remote(
            ob.at[lax.rem(j, 2), :, 1 - c],
            pr.at[lax.rem(j, 4)],
            p_s.at[lax.rem(j, 2)],
            p_r.at[lax.rem(j, 4)],
            at(dc=1),
        )

    def first_copy(j, q, outer, inner):
        dev = at(dx=inner * c, dz=inner * (1 - c))
        return remote(cs.at[lax.rem(j, 4), q], fr.at[outer, inner - 1], f_s.at[lax.rem(j, 4), q], f_r.at[outer, inner - 1], dev)

    def second_copy(outer):
        dev = at(dx=outer * (1 - c), dz=outer * c)
        return remote(own.at[outer], sr.at[outer - 1], s_s.at[outer - 1], s_r.at[outer - 1], dev)

    def place(j, q):
        dx, dz = chip(j, q)
        return jnp.where(c == 0, dx, dz), jnp.where(c == 0, dz, dx)

    def project(j):
        chips = [chip(j, q) for q in range(2)]
        core_arrival(*chips[0]).wait_recv()
        core_arrival(*chips[1]).wait_recv()
        picks = []
        for q in range(2):
            for s in range(2):
                m = toks[chips[q][0], chips[q][1], s, :, pl.ds(quarter, META)].astype(F32).T
                codes = m[:top] * cap + m[top : 2 * top]
                pick = jnp.zeros((8 * cap, tokens), F32)
                for k in range(top):
                    pick = jnp.where(rowc[2 * q + s] == codes[k : k + 1, :], 1.0, pick)
                picks.append(pick.astype(BF16))
        picks = [jnp.concatenate(picks[:2], axis=1), jnp.concatenate(picks[2:], axis=1)]

        @pl.loop(0, 2)
        def _(n):
            part = cols(n, quarter // 2)
            value = jnp.zeros((8 * cap, quarter // 2), F32)
            for q in range(2):
                data = toks[chips[q][0], chips[q][1], :, :, part].reshape(2 * tokens, quarter // 2)
                value = value + jnp.dot(picks[q], data, preferred_element_type=F32)
            xb[:, part] = value.astype(BF16)

        for l in range(2):

            @pl.loop(0, 4)
            def _(o):
                pb[lax.rem(j, 3), o, pl.ds(l * half_rows, half_rows), :] = jnp.dot(
                    xb[pl.ds(l * half_rows, half_rows), :], wg[l, o], preferred_element_type=F32
                ).astype(BF16)

        y1_copy(j, 0).start()
        y1_copy(j, 1).start()

    def relay(j):
        n = lax.rem(j, 3)
        for side in range(2):
            y1_copy(j, side).wait()
            o = lax.rem(y + 1 + 2 * side, 4)
            rows = pl.ds(side * half_rows, half_rows)
            value = pb[n, o, rows, :].astype(F32) + y1[lax.rem(j, 4), side].astype(F32)
            pb[n, o, rows, :] = value.astype(BF16)
            y2_copy(j, side).start()

    def activate(j):
        y2_copy(j, 0).wait()
        y2_copy(j, 1).wait()
        slot = lax.rem(j, 4)
        value = pb[lax.rem(j, 3), y].astype(F32) + y2[slot, 0].astype(F32) + y2[slot, 1].astype(F32)
        hb[slot, y] = (jax.nn.silu(value[:, :block]) * value[:, block:]).astype(BF16)
        for d in (1, 3, 2):
            h_copy(j, d).start()

    def expand(j):
        for d in (1, 3, 2):
            h_copy(j, d).wait_send()
            h_arrival(j, d).wait_recv()
        slot = lax.rem(j, 4)
        for l in range(2):
            lhs = jnp.concatenate([hb[slot, o, pl.ds(l * half_rows, half_rows), :] for o in range(4)], axis=1)

            @pl.loop(0, 2)
            def _(n):
                value = jnp.dot(lhs, wd[l, :, cols(n, quarter // 2)], preferred_element_type=F32)
                ob[lax.rem(j, 2), l, :, :, cols(n, quarter // 2)] = value.astype(BF16).reshape(2, 2 * cap, quarter // 2)

        p_copy(j).start()

    def gather_back(j):
        p_copy(j).wait()
        for q in range(2):
            _, inner_before = place(j - 4, q)

            @pl.when((j >= 4) & (inner_before != 0))
            def _():
                first_copy(j, q, 0, 1).wait_send()

        for q in range(2):
            dx, dz = chip(j, q)
            m = toks[dx, dz, c, :, pl.ds(quarter, META)].astype(F32)
            codes, gate = m[:, :top] * cap + m[:, top : 2 * top], m[:, 2 * top : 3 * top]
            sides = []
            for base in (e, e + 1 - 2 * c):
                rows = tab[q : q + 1, :] + (2 * cap * base).astype(F32)
                side = jnp.zeros((tokens, 4 * cap), F32)
                for k in range(top):
                    side = jnp.where(codes[:, k : k + 1] == rows, gate[:, k : k + 1], side)
                sides.append(side.astype(BF16))

            @pl.loop(0, 2)
            def _(n):
                part = cols(n, quarter // 2)
                here = ob[lax.rem(j, 2), :, c, :, part].reshape(4 * cap, quarter // 2)
                other = pr[lax.rem(j, 4), :, :, part].reshape(4 * cap, quarter // 2)
                value = jnp.dot(sides[0], here, preferred_element_type=F32)
                value = value + jnp.dot(sides[1], other, preferred_element_type=F32)
                cs[lax.rem(j, 4), q, :, part] = value.astype(BF16)

            outer, inner = place(j, q)

            @pl.when(inner == 0)
            def _():
                own[outer] = cs[lax.rem(j, 4), q]

            @pl.when(inner != 0)
            def _():
                first_copy(j, q, outer, inner).start()

    def combine(outer):
        value = own[outer].astype(F32)
        for inner in (1, 2, 3):
            first_copy(0, 0, outer, inner).wait_recv()
            value = value + fr[outer, inner - 1].astype(F32)
        return value

    def finish(outer):
        own[outer] = combine(outer).astype(BF16)
        second_copy(outer).start()

    @pl.loop(0, STEPS + 4)
    def _(it):
        @pl.when(it < STEPS)
        def _():
            project(it)

        @pl.when((it >= 1) & (it <= STEPS))
        def _():
            relay(it - 1)

        @pl.when((it >= 3) & (it <= STEPS + 1))
        def _():
            activate(it - 2)

        @pl.when(it == 1)
        def _():
            ag_first(2).wait_recv()
            ag_second(2, 1).start()
            ag_second(2, 3).start()
            pass_on(0, 0).start()
            pass_on(0, 1).start()

        @pl.when((it >= 1) & (it + 1 < STEPS))
        def _():
            service(it + 1)

        @pl.when(it == 1)
        def _():
            activate(0)

        @pl.when(it == 2)
        def _():
            for a in (1, 3):
                pass_on(a, 0).start()
                pass_on(a, 1).start()

        @pl.when(it == 4)
        def _():
            pass_on(2, 0).start()
            pass_on(2, 1).start()

        @pl.when((it >= 3) & (it <= STEPS + 2))
        def _():
            expand(it - 3)

        @pl.when(it >= 4)
        def _():
            gather_back(it - 4)

        @pl.when((c == 0) & (it == 10))
        def _():
            finish(1)
            finish(3)

    @pl.when(c == 1)
    def _():
        finish(1)
        finish(3)

    finish(2)
    value = stream[...].astype(F32) + combine(0)
    for outer in (1, 3, 2):
        second_copy(outer).wait()
        value = value + sr[outer - 1].astype(F32)
    out[...] = value.astype(BF16)

    for side in range(2):
        attn_first(side).wait_send()
    for d in (1, 2, 3):
        ss_copy(d).wait_send()
        ag_first(d).wait_send()
    for a in range(4):
        ag_second(a, 1).wait_send()
        ag_second(a, 3).wait_send()
        pass_on(a, 0).wait_send()
        pass_on(a, 1).wait_send()
        for b in range(4):
            core_copy(a, b).wait_send()
    for j in range(STEPS - 4, STEPS):
        for q in range(2):
            _, inner = place(j, q)

            @pl.when(inner != 0)
            def _():
                first_copy(j, q, 0, 1).wait_send()


def per_device(attn_partials, residual, norm_gain, gate_up, down, expert_ids, gate_ints):
    tokens, width = residual.shape
    quarter = norm_gain.shape[0]
    local, _, double = gate_up.shape
    hidden = down.shape[1]
    block = hidden // 4
    groups = lax.axis_size("expert")
    top = expert_ids.shape[1]
    cap = 3 * tokens * top // (2 * groups * local)
    rows = 8 * cap
    dma = pltpu.SemaphoreType.DMA
    vmem = pl.BlockSpec(memory_space=pltpu.VMEM)
    anywhere = pl.BlockSpec(memory_space=pl.ANY)
    scratch = [
        pltpu.VMEM((local, 4, quarter, 2 * block), BF16),
        pltpu.VMEM((local, hidden, quarter), BF16),
        pltpu.VMEM((4, 4, 2, tokens, quarter + META), BF16),
        pltpu.VMEM((4, rows, tokens), F32),
        pltpu.VMEM((3, 4, rows, 2 * block), BF16),
        pltpu.VMEM((rows, quarter), BF16),
        pltpu.VMEM((4, 2, rows // 2, 2 * block), BF16),
        pltpu.VMEM((4, 2, rows, 2 * block), BF16),
        pltpu.VMEM((4, 4, rows, block), BF16),
        pltpu.VMEM((2, local, 2, 2 * cap, quarter), BF16),
        pltpu.VMEM((4, local, 2 * cap, quarter), BF16),
        pltpu.VMEM((4, tokens, quarter), BF16),
        pltpu.VMEM((4, 2, tokens, quarter), BF16),
        pltpu.VMEM((4, 3, tokens, quarter), BF16),
        pltpu.VMEM((3, tokens, quarter), BF16),
        pltpu.VMEM((tokens, quarter), BF16),
        pltpu.VMEM((4, 8, tokens), F32),
        dma((18,)),
        dma((4,)),
        dma((2,)),
        dma((2,)),
        dma((2,)),
        dma((2,)),
        dma((3,)),
        dma((3,)),
        dma((4,)),
        dma((4,)),
        dma((4, 4)),
        dma((4, 4)),
        dma((4, 2)),
        dma((4, 2)),
        dma((4, 4)),
        dma((4, 4)),
        dma((3, 2)),
        dma((4, 2)),
        dma((3, 2)),
        dma((4, 2)),
        dma((4, 3)),
        dma((4, 3)),
        dma((2,)),
        dma((4,)),
        dma((4, 2)),
        dma((4, 3)),
        dma((3,)),
        dma((3,)),
    ]
    return pl.pallas_call(
        functools.partial(layer_kernel, cap, groups * local),
        out_shape=jax.ShapeDtypeStruct((tokens, quarter), BF16),
        in_specs=[anywhere, anywhere, vmem, anywhere, anywhere, vmem, vmem, vmem],
        out_specs=vmem,
        scratch_shapes=scratch,
        compiler_params=pltpu.CompilerParams(collective_id=0, has_side_effects=True, vmem_limit_bytes=63 * 2**20),
        cost_estimate=pl.CostEstimate(flops=30 * 10**9, bytes_accessed=30 * 10**6, transcendentals=0),
    )(
        attn_partials[0],
        residual,
        norm_gain,
        gate_up,
        down,
        expert_ids.T,
        gate_ints.T,
        jnp.asarray(row_table(cap)),
    )


def solution(mesh):
    in_specs = (
        P("tensor", "expert", None),
        P("expert", None),
        P("tensor"),
        P("expert", "tensor", None),
        P("expert", None, "tensor"),
        P("expert", None),
        P("expert", None),
    )
    return jax.shard_map(
        per_device, mesh=mesh, in_specs=in_specs, out_specs=P("expert", "tensor"), check_vma=False
    )
```
